32 devices in a mesh: rep: 8 (over y, x, core), shard: 4 (over z).
Axes of the slice: x: 2, y: 2, z: 4, core: 2. Of those that a mesh axis runs over, the one named last changes fastest.
Arguments:
- tokens: float32 [32768, 768], P(('rep', 'shard')), may hold values from -6 to 6
- cotangent: float32 [32768, 768], P(('rep', 'shard')), may hold values from -6 to 6
- lengths: int32 [32, 8], P(('rep', 'shard')), may hold values from 0 to 1024, as said below
- proj_weight: float32 [768, 3352], P('shard'), may hold values from -0.21875 to 0.21875
- proj_first: float32 [768, 3352], P('shard'), as said below
- proj_second: float32 [768, 3352], P('shard'), as said below
- out_weight: float32 [1536, 768], P('shard'), may hold values from -0.15625 to 0.15625
- out_first: float32 [1536, 768], P('shard'), as said below
- out_second: float32 [1536, 768], P('shard'), as said below
- small_params: float32 [11336], P('shard'), as said below
- small_first: float32 [11336], P('shard'), as said below
- small_second: float32 [11336], P('shard'), as said below
Outputs:
- block_out: float32 [32768, 768], P(('rep', 'shard'))
- token_grad: float32 [32768, 768], P(('rep', 'shard'))
- proj_new: float32 [768, 3352], P('shard')
- proj_first_new: float32 [768, 3352], P('shard')
- proj_second_new: float32 [768, 3352], P('shard')
- out_new: float32 [1536, 768], P('shard')
- out_first_new: float32 [1536, 768], P('shard')
- out_second_new: float32 [1536, 768], P('shard')
- small_new: float32 [11336], P('shard')
- small_first_new: float32 [11336], P('shard')
- small_second_new: float32 [11336], P('shard')
The draws below stay inside these ranges and needn't reach their ends.
Inputs may be any that keep to these rules, and one draw needn't show every extreme that they name: Each row lists the lengths of the sequences of one pack, zeros allowed; a row sums to at most 1024 and to at least 256; in every draw some row holds one sequence of exactly 1024. `small_params`: gains within 0.6 to 1.4, convolution weights within -0.9 to 0.9, convolution bias within -0.5 to 0.5, step bias within -7 to -2.2, log decay rates within 0 to log 16, skip gains within 0.5 to 1.5. `proj_first`: both signs. `proj_second`: Positive. `out_first`: both signs. `out_second`: Positive. `small_first`: both signs. `small_second`: Positive.
All inputs are finite; a program needn't handle non-finite values.
Results may differ from the reference program's by a relative error of at most 0.012.
The reference program's roundings to bfloat16 on the way count: a program that leaves them out, or rounds other values in their place, can miss the bound.
Values may be sent and summed in bfloat16 or wider, within the bound.
A program may use at most 448 MiB of HBM per device.

```python
import math
import jax
import jax.numpy as jnp
from jax import lax

D = 768
P_SIZE = 64
N = 128
K = 4
TOK_DEV = 1024
SEQS = 8
STEP = 10
DI = 1536
H = 24
CH = 1792
PROJ = 3352
NV = 11336
TOKENS = 32768


def bounded(key, shape, spread):
    return spread * jax.random.uniform(key, shape, jnp.float32, -1.7320508, 1.7320508)


def second_law(key, shape, level):
    return level * jnp.exp(jax.random.uniform(key, shape, jnp.float32, 0.0, math.log(4.0)))


def draw_lengths(key, part):
    key = jax.random.fold_in(key, 11)
    keys = jax.random.split(key, 3)
    packs = TOKENS // TOK_DEV
    live_tok = jax.random.randint(keys[0], (packs,), TOK_DEV // 4, 3 * TOK_DEV // 4 + 1)
    cuts = jax.random.randint(keys[1], (packs, SEQS - 1), 0, live_tok[:, None] + 1)
    cuts = jnp.sort(cuts, axis=1)
    edges = jnp.concatenate([jnp.zeros((packs, 1), jnp.int32), cuts, live_tok[:, None]], axis=1)
    spans = edges[:, 1:] - edges[:, :-1]
    single = jnp.zeros((SEQS,), jnp.int32).at[0].set(TOK_DEV)
    fullest = jax.random.randint(keys[2], (), 0, packs)
    chosen = (jnp.arange(packs) == fullest)[:, None]
    return jnp.where(chosen, single[None, :], spans).astype(jnp.int32)


def draw_small_params(key, part):
    key = jax.random.fold_in(key, 31)
    keys = jax.random.split(key, 7)
    gain_in = jax.random.uniform(keys[0], (D,), jnp.float32, 0.6, 1.4)
    conv_flat = jax.random.uniform(keys[1], (K * CH,), jnp.float32, -0.9, 0.9)
    conv_bias = jax.random.uniform(keys[2], (CH,), jnp.float32, -0.5, 0.5)
    step_init = jnp.exp(jax.random.uniform(keys[3], (H,), jnp.float32, math.log(0.001), math.log(0.1)))
    step_bias = step_init + jnp.log(-jnp.expm1(-step_init))
    rate_log = jnp.log(jax.random.uniform(keys[4], (H,), jnp.float32, 1.0, 16.0))
    skip_gain = jax.random.uniform(keys[5], (H,), jnp.float32, 0.5, 1.5)
    gain_out = jax.random.uniform(keys[6], (DI,), jnp.float32, 0.6, 1.4)
    return jnp.concatenate([gain_in, conv_flat, conv_bias, step_bias, rate_log, skip_gain, gain_out])


def draw_proj_first(key, part):
    key = jax.random.fold_in(key, 21)
    return bounded(key, (D, PROJ), math.sqrt(0.1 * TOKENS) / 9.0)


def draw_proj_second(key, part):
    key = jax.random.fold_in(key, 22)
    return second_law(key, (D, PROJ), 0.1 * TOKENS / 19.0)


def draw_out_first(key, part):
    key = jax.random.fold_in(key, 23)
    return bounded(key, (DI, D), math.sqrt(0.5 * TOKENS) / 9.0)


def draw_out_second(key, part):
    key = jax.random.fold_in(key, 24)
    return second_law(key, (DI, D), 0.5 * TOKENS / 19.0)


def draw_small_first(key, part):
    key = jax.random.fold_in(key, 25)
    return bounded(key, (NV,), math.sqrt(0.3 * TOKENS) / 9.0)


def draw_small_second(key, part):
    key = jax.random.fold_in(key, 26)
    return second_law(key, (NV,), 0.3 * TOKENS / 19.0)


def steps_of(stream_key, shape, cuts, low, high):
    def one(axis_at, shards_of):
        draws = jax.random.uniform(jax.random.fold_in(jax.random.fold_in(stream_key, 6), axis_at), (shards_of,), jnp.float32, low / len(cuts), high / len(cuts))
        return jnp.repeat(jnp.exp(draws), shape[axis_at] // shards_of).reshape((-1,) + (1,) * (len(shape) - axis_at - 1))

    level = one(*cuts[0])
    for cut in cuts[1:]:
        level = level * one(*cut)
    return level


def noise(rng, shape, scale, limit, shards=(), kind=jnp.bfloat16):
    loudness = steps_of(rng, shape, shards, -0.22, 0.18) if shards else 1.0
    array = jax.random.normal(rng, shape, jnp.float32) * scale * loudness
    return jnp.minimum(jnp.maximum(array, -limit), limit).astype(kind)


def setup_inputs(seed: int = 0) -> dict:
    splits = jax.random.split(jax.random.key(seed), 13)
    tokens = noise(splits[0], (TOKENS, D), 1.0, 6.0, ((0, 32),), jnp.float32)
    cotangent = noise(splits[1], (TOKENS, D), 1.0, 6.0, ((0, 32),), jnp.float32)
    lengths = draw_lengths(jax.random.fold_in(splits[12], 71), 0)
    proj_weight = noise(splits[3], (D, PROJ), D ** -0.5, 0.21875, ((0, 4),), jnp.float32)
    proj_first = draw_proj_first(jax.random.fold_in(splits[12], 71), 0)
    proj_second = draw_proj_second(jax.random.fold_in(splits[12], 71), 0)
    out_weight = noise(splits[6], (DI, D), DI ** -0.5, 0.15625, ((0, 4),), jnp.float32)
    out_first = draw_out_first(jax.random.fold_in(splits[12], 71), 0)
    out_second = draw_out_second(jax.random.fold_in(splits[12], 71), 0)
    small_params = draw_small_params(jax.random.fold_in(splits[12], 71), 0)
    small_first = draw_small_first(jax.random.fold_in(splits[12], 71), 0)
    small_second = draw_small_second(jax.random.fold_in(splits[12], 71), 0)
    return {"tokens": tokens, "cotangent": cotangent, "lengths": lengths, "proj_weight": proj_weight, "proj_first": proj_first, "proj_second": proj_second, "out_weight": out_weight, "out_first": out_first, "out_second": out_second, "small_params": small_params, "small_first": small_first, "small_second": small_second}


EPS_NORM = 1e-05
BETA_ONE = 0.9
BETA_TWO = 0.95
ADAM_EPS = 1e-08
DECAY_WEIGHT = 0.1
RATE_PROJ = 0.03
RATE_OUT = 0.02
RATE_SMALL = 0.4
highest = lax.Precision.HIGHEST

@jax.custom_vjp
def low(v):
    return lax.optimization_barrier(v.astype(jnp.bfloat16)).astype(jnp.float32)

@jax.custom_vjp
def low_back(v):
    return v

def low_keep(v):
    return (low(v), None)

def low_pass(kept, grad):
    return (grad,)

def back_keep(v):
    return (v, None)

def back_low(kept, grad):
    return (low(grad),)
low.defvjp(low_keep, low_pass)
low_back.defvjp(back_keep, back_low)

def unpack(small):
    offset = 0
    pieces = []
    for extent in (D, K * CH, CH, H, H, H, DI):
        pieces.append(small[offset:offset + extent])
        offset = offset + extent
    return (pieces[0], pieces[1].reshape(K, CH), pieces[2], pieces[3], pieces[4], pieces[5], pieces[6])

def segments(row_lengths):
    edges = jnp.cumsum(row_lengths).astype(jnp.int32)
    places = jnp.arange(TOK_DEV, dtype=jnp.int32)
    segment = lax.optimization_barrier(jnp.sum((places[:, None] >= edges[None, :]).astype(jnp.int32), axis=1))
    live_rows = (places < edges[-1]).astype(jnp.float32)
    return (segment, live_rows)

def convolve(conv_in, conv_weight, conv_bias, segment):
    row_count = conv_in.shape[0]
    total_sum = conv_bias + conv_weight[K - 1] * conv_in
    for shift_by in range(1, K):
        shifted = jnp.concatenate([jnp.zeros((shift_by, conv_in.shape[1]), conv_in.dtype), conv_in[:row_count - shift_by]], axis=0)
        earlier = jnp.concatenate([jnp.full((shift_by,), -1, jnp.int32), segment[:row_count - shift_by]], axis=0)
        same_seg = (earlier == segment).astype(conv_in.dtype)
        total_sum = total_sum + conv_weight[K - 1 - shift_by] * shifted * same_seg[:, None]
    return jax.nn.silu(total_sum)

def mixer(projected, params, segment):
    conv_weight, conv_bias, step_bias, rate_log, skip_gain, gain_out = params[1:]
    gate_z = projected[:, :DI]
    conv_in = projected[:, DI:DI + CH]
    step_raw = projected[:, DI + CH:]
    active = convolve(conv_in, conv_weight, conv_bias, segment)
    row_count = active.shape[0]
    values = active[:, :DI].reshape(row_count, H, P_SIZE)
    key_b = active[:, DI:DI + N]
    query_c = active[:, DI + N:]
    step_size = jax.nn.softplus(step_raw + step_bias)
    decay_log = -step_size * jnp.exp(rate_log)
    running = jnp.cumsum(decay_log, axis=0).T
    places = jnp.arange(row_count)
    allowed = (places[None, :] <= places[:, None]) & (segment[None, :] == segment[:, None])
    spread_log = running[:, :, None] - running[:, None, :]
    factor = jnp.where(allowed[None], jnp.exp(jnp.where(allowed[None], spread_log, 0.0)), 0.0)
    scores = jnp.dot(query_c, key_b.T, precision=highest)
    weights = factor * scores[None] * step_size.T[:, None, :]
    output = jnp.einsum('hts,shp->thp', weights, values, precision=highest) + skip_gain[None, :, None] * values
    output = output.reshape(row_count, DI)
    gated = output * jax.nn.silu(gate_z)
    inv_rms = lax.rsqrt(lax.optimization_barrier(jnp.mean(gated * gated, axis=1, keepdims=True)) + EPS_NORM)
    return gated * inv_rms * gain_out

def pack_forward(proj_low, out_low, small_low, rows_in, row_lengths):
    params = unpack(small_low)
    segment, live_rows = segments(row_lengths)
    inv_rms = lax.rsqrt(lax.optimization_barrier(jnp.mean(rows_in * rows_in, axis=1, keepdims=True)) + EPS_NORM)
    normed = low(rows_in * inv_rms * params[0])
    projected = low_back(jnp.dot(normed, proj_low, precision=highest))
    mixed = low(mixer(projected, params, segment))
    branch = low_back(jnp.dot(mixed, out_low, precision=highest))
    return rows_in + live_rows[:, None] * branch

def forward(tokens, proj_weight, out_weight, small_params, lengths):
    proj_low = low(proj_weight)
    out_low = low(out_weight)
    small_low = low(small_params)
    packed = tokens.reshape(-1, TOK_DEV, D)
    step_fn = jax.checkpoint(pack_forward)

    def one_pack(carry_in, inputs):
        return (carry_in, step_fn(proj_low, out_low, small_low, inputs[0], inputs[1]))
    unused, outputs = lax.scan(one_pack, jnp.zeros((), jnp.float32), (packed, lengths))
    return outputs.reshape(-1, D)

def adam(weight, first, second, grad_sum, step_rate, decay_on):
    first_new = BETA_ONE * first + (1.0 - BETA_ONE) * grad_sum
    second_new = BETA_TWO * second + (1.0 - BETA_TWO) * grad_sum * grad_sum
    first_hat = first_new / (1.0 - BETA_ONE ** STEP)
    second_hat = second_new / (1.0 - BETA_TWO ** STEP)
    weight_new = weight - step_rate * (first_hat / (jnp.sqrt(second_hat) + ADAM_EPS) + decay_on * weight)
    return (weight_new, first_new, second_new)

def reference(tokens, cotangent, lengths, proj_weight, proj_first, proj_second, out_weight, out_first, out_second, small_params, small_first, small_second):

    def inner_fn(tok_in, proj_in, out_in, small_in):
        return forward(tok_in, proj_in, out_in, small_in, lengths)
    block_out, pullback = jax.vjp(inner_fn, tokens, proj_weight, out_weight, small_params)
    token_grad, proj_grad, out_grad, small_grad = pullback(cotangent)
    proj_new, proj_first_new, proj_second_new = adam(proj_weight, proj_first, proj_second, proj_grad, RATE_PROJ, DECAY_WEIGHT)
    out_new, out_first_new, out_second_new = adam(out_weight, out_first, out_second, out_grad, RATE_OUT, DECAY_WEIGHT)
    small_new, small_first_new, small_second_new = adam(small_params, small_first, small_second, small_grad, RATE_SMALL, 0.0)
    return (block_out, token_grad, proj_new, proj_first_new, proj_second_new, out_new, out_first_new, out_second_new, small_new, small_first_new, small_second_new)
```

```python
import functools

import jax
import jax.numpy as jnp
from jax import lax
from jax.experimental import pallas as pl
from jax.experimental.pallas import tpu as pltpu
from jax.sharding import PartitionSpec as P

D = 768
P_SIZE = 64
N = 128
K = 4
STEP = 10
DI = 1536
H = 24
CH = 1792
PROJ = 3352
WIDE = 3456
LANES = 128
L = 128
PAIRS = H // 2
TAIL = 8
FAR = -1e30
VMEM_BYTES = 56 * 1024 * 1024

EPS_NORM = 1e-05
BETA_ONE = 0.9
BETA_TWO = 0.95
ADAM_EPS = 1e-08
DECAY_WEIGHT = 0.1
RATE_PROJ = 0.03
RATE_OUT = 0.02
RATE_SMALL = 0.4
highest = lax.Precision.HIGHEST
f32 = jnp.float32
bf16 = jnp.bfloat16

CARRIED, KEPT, SAME, LATER = 0, 1, 2, 5


def dot(a, b, contract=((1,), (0,))):
    return lax.dot_general(a, b, (contract, ((), ())), preferred_element_type=f32)


def split(x):
    high = x.astype(bf16)
    return high, (x - high.astype(f32)).astype(bf16)


def expand(x, heads):
    high, low = split(x)
    return dot(high, heads) + dot(low, heads)


def head_sums(x, heads):
    high, low = split(x)
    return dot(high, heads, ((1,), (1,))) + dot(low, heads, ((1,), (1,)))


def sigmoid(x):
    return 1.0 / (1.0 + jnp.exp(-x))


def softplus(x):
    return jnp.maximum(x, 0.0) + jnp.log1p(jnp.exp(-jnp.abs(x)))


def triangle(lower):
    rows = lax.broadcasted_iota(jnp.int32, (L, L), 0)
    cols = lax.broadcasted_iota(jnp.int32, (L, L), 1)
    return (cols <= rows if lower else cols >= rows).astype(f32)


def conv_pre(ext_ref, flags, conv_w, conv_b):
    pre = conv_b + conv_w[K - 1 : K] * ext_ref[TAIL : TAIL + L]
    for shift_by in range(1, K):
        same = flags[:, SAME + shift_by - 1 : SAME + shift_by]
        pre = pre + conv_w[K - 1 - shift_by : K - shift_by] * (
            ext_ref[TAIL - shift_by : TAIL - shift_by + L] * same
        )
    return pre


def decays(step_raw, flags, stay, step_bias, rate):
    step = softplus(step_raw + step_bias)
    decay_log = -step * rate
    running = jnp.dot(triangle(True), decay_log, precision=highest, preferred_element_type=f32)
    last = running[L - 1 : L]
    reach = jnp.exp(running) * flags[:, CARRIED : CARRIED + 1]
    keep = jnp.exp(last - running) * flags[:, KEPT : KEPT + 1]
    stay_w = jnp.exp(last) * stay
    return step, decay_log, running, reach, keep, stay_w


def far_mask(seg_col, seg_row):
    rows = lax.broadcasted_iota(jnp.int32, (L, L), 0)
    cols = lax.broadcasted_iota(jnp.int32, (L, L), 1)
    return jnp.where((cols <= rows) & (seg_col == seg_row), 0.0, FAR)


def halves(pair):
    left = lax.broadcasted_iota(jnp.int32, pair.shape, 1) < P_SIZE
    zero = jnp.zeros_like(pair)
    return jnp.concatenate([jnp.where(left, pair, zero), jnp.where(left, zero, pair)], axis=0)


def forward_kernel(
    proj_ref, flags_ref, segc_ref, segr_ref, stay_ref, conv_w_ref, conv_b_ref, step_b_ref,
    rate_ref, skip_ref, gain_ref, heads_ref,
    mixed_ref, y_ref, states_ref, tails_ref,
    ext_ref, state_ref,
):
    @pl.when(pl.program_id(0) == 0)
    def _():
        ext_ref[L : L + TAIL] = jnp.zeros((TAIL, CH), f32)
        state_ref[...] = jnp.zeros((N, DI), f32)

    flags = flags_ref[...]
    heads = heads_ref[...]
    tail = ext_ref[L : L + TAIL]
    ext_ref[0:TAIL] = tail
    tails_ref[...] = tail
    ext_ref[TAIL : TAIL + L] = proj_ref[:, DI : DI + CH]
    pre = conv_pre(ext_ref, flags, conv_w_ref[...], conv_b_ref[...])
    active = pre * sigmoid(pre)
    values = active[:, :DI]
    keys = active[:, DI : DI + N].astype(bf16)
    query = active[:, DI + N :].astype(bf16)
    step, _, running, reach, keep, stay_w = decays(
        proj_ref[:, DI + CH :], flags, stay_ref[0], step_b_ref[...], rate_ref[...]
    )
    run_t = running.T
    far = far_mask(segc_ref[...], segr_ref[0])
    scores = dot(query, keys, ((1,), (1,)))
    scaled = (values * expand(step, heads)).astype(bf16)
    state = state_ref[...]
    states_ref[0] = state
    outer = dot(query, state.astype(bf16)) * expand(reach, heads)
    inner = []
    for pair in range(PAIRS):
        weights = []
        for h in (2 * pair, 2 * pair + 1):
            factor = jnp.exp(running[:, h : h + 1] - run_t[h : h + 1, :] + far)
            weights.append((factor * scores).astype(bf16))
        stacked = halves(scaled[:, pair * LANES : (pair + 1) * LANES])
        inner.append(dot(jnp.concatenate(weights, axis=1), stacked))
    y = jnp.concatenate(inner, axis=1) + outer + skip_ref[...] * values
    y_ref[...] = y
    fresh = (values * expand(keep * step, heads)).astype(bf16)
    state_ref[...] = state * expand(jnp.broadcast_to(stay_w, (8, LANES)), heads)[0:1] + dot(
        keys, fresh, ((0,), (0,))
    )
    gate = proj_ref[:, :DI]
    gated = y * (gate * sigmoid(gate))
    inv_rms = lax.rsqrt(jnp.mean(gated * gated, axis=1, keepdims=True) + EPS_NORM)
    mixed_ref[...] = (gated * inv_rms * gain_ref[...]).astype(bf16)


def backward_kernel(
    proj_ref, dmix_ref, y_ref, states_ref, tails_ref, flags_ref, segc_ref, segr_ref, stay_ref,
    conv_w_ref, conv_b_ref, step_b_ref, rate_ref, skip_ref, gain_ref, heads_ref,
    dproj_ref, gconv_ref, ghead_ref, gwide_ref,
    ext_ref, dext_ref, dstate_ref, cross_ref,
):
    @pl.when(pl.program_id(0) == 0)
    def _():
        dext_ref[0:TAIL] = jnp.zeros((TAIL, CH), f32)
        dstate_ref[...] = jnp.zeros((N, DI), f32)
        cross_ref[...] = jnp.zeros((8, LANES), f32)
        gconv_ref[...] = jnp.zeros((8, CH), f32)
        ghead_ref[...] = jnp.zeros((8, LANES), f32)
        gwide_ref[...] = jnp.zeros((8, DI), f32)

    flags = flags_ref[...]
    heads = heads_ref[...]
    skip = skip_ref[...]
    rate = rate_ref[...]
    ext_ref[0:TAIL] = tails_ref[...]
    ext_ref[TAIL : TAIL + L] = proj_ref[:, DI : DI + CH]
    pre = conv_pre(ext_ref, flags, conv_w_ref[...], conv_b_ref[...])
    sig = sigmoid(pre)
    active = pre * sig
    values = active[:, :DI]
    keys = active[:, DI : DI + N].astype(bf16)
    query = active[:, DI + N :].astype(bf16)
    step_in = proj_ref[:, DI + CH :]
    step, decay_log, running, reach, keep, stay_w = decays(
        step_in, flags, stay_ref[0], step_b_ref[...], rate
    )

    gate = proj_ref[:, :DI]
    y = y_ref[...]
    dmix = dmix_ref[...]
    gate_sig = sigmoid(gate)
    silu = gate * gate_sig
    gated = y * silu
    inv_rms = lax.rsqrt(jnp.mean(gated * gated, axis=1, keepdims=True) + EPS_NORM)
    gwide_ref[0:1] += jnp.sum(dmix * (gated * inv_rms), axis=0, keepdims=True)
    q = dmix * gain_ref[...]
    slope = inv_rms * inv_rms * inv_rms * jnp.mean(q * gated, axis=1, keepdims=True)
    dgated = inv_rms * q - gated * slope
    dy = dgated * silu
    dproj_ref[:, :DI] = (dgated * y * (gate_sig * (1.0 + gate * (1.0 - gate_sig)))).astype(bf16)
    gwide_ref[1:2] += jnp.sum(dy * values, axis=0, keepdims=True)

    run_t = running.T
    far = far_mask(segc_ref[...], segr_ref[0])
    scores = dot(query, keys, ((1,), (1,)))
    step_wide = expand(step, heads)
    scaled = (values * step_wide).astype(bf16)
    dy_low = dy.astype(bf16)
    lane = lax.broadcasted_iota(jnp.int32, (L, LANES), 1)
    left = lane < P_SIZE
    f_sum = jnp.zeros((L, L), f32)
    row_sums = jnp.zeros((L, LANES), f32)
    col_sums = []
    inner = []
    for pair in range(PAIRS):
        columns = slice(pair * LANES, (pair + 1) * LANES)
        dy_pair = dy_low[:, columns]
        grads = dot(dy_pair, halves(scaled[:, columns]), ((1,), (1,)))
        weights = []
        for half in range(2):
            h = 2 * pair + half
            factor = jnp.exp(running[:, h : h + 1] - run_t[h : h + 1, :] + far)
            weight = factor * scores
            grad = grads[:, half * L : (half + 1) * L]
            f_sum = f_sum + grad * factor
            e = grad * weight
            row_sums = jnp.where(lane == h, jnp.sum(e, axis=1, keepdims=True), row_sums)
            col_sums.append(jnp.sum(e, axis=0, keepdims=True))
            weights.append(weight.astype(bf16))
        both = dot(jnp.concatenate(weights, axis=1), dy_pair, ((0,), (0,)))
        inner.append(jnp.where(left, both[:L], both[L:]))
    col_sums.append(jnp.zeros((LANES - H, L), f32))
    col_sum = jnp.concatenate(col_sums, axis=0).T
    f_low = f_sum.astype(bf16)

    state = states_ref[0]
    state_low = state.astype(bf16)
    dstate = dstate_ref[...]
    dstate_low = dstate.astype(bf16)
    reach_wide = expand(reach, heads)
    keep_wide = expand(keep, heads)
    dy_reach = dy * reach_wide
    dy_reach_low = dy_reach.astype(bf16)
    row_in = head_sums(dy_reach * dot(query, state_low), heads)
    u_out = dot(keys, dstate_low) * keep_wide
    u_all = jnp.concatenate(inner, axis=1) + u_out
    fresh = (values * (keep_wide * step_wide)).astype(bf16)
    dquery = dot(f_low, keys) + dot(dy_reach_low, state_low, ((1,), (1,)))
    dkeys = dot(f_low, query, ((0,), (0,))) + dot(fresh, dstate_low, ((1,), (1,)))
    dvalues = u_all * step_wide + skip * dy
    out_sum = head_sums(values * u_out, heads)
    dstep_own = head_sums(values * u_all, heads)
    drunning = row_sums - col_sum + row_in - step * out_sum
    ddecay = cross_ref[0:1] + jnp.dot(
        triangle(False), drunning, precision=highest, preferred_element_type=f32
    )
    dstate_new = dot(query, dy_reach_low, ((0,), (0,))) + dstate * expand(
        jnp.broadcast_to(stay_w, (8, LANES)), heads
    )[0:1]
    dstate_ref[...] = dstate_new
    cross_ref[...] = head_sums(
        jnp.broadcast_to(jnp.sum(dstate_new * state, axis=0, keepdims=True), (8, DI)), heads
    )
    dstep_raw = (dstep_own - rate * ddecay) * sigmoid(step_in + step_b_ref[...])
    ghead_ref[0:1] += jnp.sum(dstep_raw, axis=0, keepdims=True)
    ghead_ref[1:2] += jnp.sum(ddecay * decay_log, axis=0, keepdims=True)
    dproj_ref[:, DI + CH :] = dstep_raw.astype(bf16)

    dactive = jnp.concatenate([dvalues, dkeys, dquery], axis=1)
    dpre = dactive * (sig * (1.0 + pre * (1.0 - sig)))
    dext_ref[L : L + TAIL] = dext_ref[0:TAIL]
    dext_ref[0:L] = dpre
    conv_w = conv_w_ref[...]
    dconv = conv_w[K - 1 : K] * dpre
    gconv_ref[K : K + 1] += jnp.sum(dpre, axis=0, keepdims=True)
    gconv_ref[K - 1 : K] += jnp.sum(dpre * ext_ref[TAIL : TAIL + L], axis=0, keepdims=True)
    for shift_by in range(1, K):
        tap = K - 1 - shift_by
        same = flags[:, SAME + shift_by - 1 : SAME + shift_by]
        later = flags[:, LATER + shift_by - 1 : LATER + shift_by]
        dconv = dconv + conv_w[tap : tap + 1] * (dext_ref[shift_by : shift_by + L] * later)
        gconv_ref[tap : tap + 1] += jnp.sum(
            dpre * (ext_ref[TAIL - shift_by : TAIL - shift_by + L] * same), axis=0, keepdims=True
        )
    dproj_ref[:, DI : DI + CH] = dconv.astype(bf16)


def whole(shape):
    return pl.BlockSpec(shape, lambda i: (0,) * len(shape))


def run_forward(projected, marks, consts):
    rows = projected.shape[0]
    blocks = rows // L
    row = lambda i: (i, 0)
    deep = lambda i: (i, 0, 0)
    return pl.pallas_call(
        forward_kernel,
        grid=(blocks,),
        in_specs=[
            pl.BlockSpec((L, WIDE), row),
            pl.BlockSpec((L, 8), row),
            pl.BlockSpec((L, 1), row),
            pl.BlockSpec((1, 1, L), deep),
            pl.BlockSpec((1, 1, LANES), deep),
        ]
        + [whole(c.shape) for c in consts],
        out_specs=[
            pl.BlockSpec((L, DI), row),
            pl.BlockSpec((L, DI), row),
            pl.BlockSpec((1, N, DI), deep),
            pl.BlockSpec((TAIL, CH), row),
        ],
        out_shape=[
            jax.ShapeDtypeStruct((rows, DI), bf16),
            jax.ShapeDtypeStruct((rows, DI), f32),
            jax.ShapeDtypeStruct((blocks, N, DI), f32),
            jax.ShapeDtypeStruct((blocks * TAIL, CH), f32),
        ],
        scratch_shapes=[pltpu.VMEM((L + TAIL, CH), f32), pltpu.VMEM((N, DI), f32)],
        compiler_params=pltpu.CompilerParams(vmem_limit_bytes=VMEM_BYTES),
        name="mixer_forward",
    )(projected, *marks, *consts)


def run_backward(projected, dmix, y, states, tails, marks, consts):
    rows = projected.shape[0]
    blocks = rows // L
    row = lambda i: (blocks - 1 - i, 0)
    deep = lambda i: (blocks - 1 - i, 0, 0)
    return pl.pallas_call(
        backward_kernel,
        grid=(blocks,),
        in_specs=[
            pl.BlockSpec((L, WIDE), row),
            pl.BlockSpec((L, DI), row),
            pl.BlockSpec((L, DI), row),
            pl.BlockSpec((1, N, DI), deep),
            pl.BlockSpec((TAIL, CH), row),
            pl.BlockSpec((L, 8), row),
            pl.BlockSpec((L, 1), row),
            pl.BlockSpec((1, 1, L), deep),
            pl.BlockSpec((1, 1, LANES), deep),
        ]
        + [whole(c.shape) for c in consts],
        out_specs=[
            pl.BlockSpec((L, WIDE), row),
            whole((8, CH)),
            whole((8, LANES)),
            whole((8, DI)),
        ],
        out_shape=[
            jax.ShapeDtypeStruct((rows, WIDE), bf16),
            jax.ShapeDtypeStruct((8, CH), f32),
            jax.ShapeDtypeStruct((8, LANES), f32),
            jax.ShapeDtypeStruct((8, DI), f32),
        ],
        scratch_shapes=[
            pltpu.VMEM((L + TAIL, CH), f32),
            pltpu.VMEM((L + TAIL, CH), f32),
            pltpu.VMEM((N, DI), f32),
            pltpu.VMEM((8, LANES), f32),
        ],
        compiler_params=pltpu.CompilerParams(vmem_limit_bytes=VMEM_BYTES),
        name="mixer_backward",
    )(projected, dmix, y, states, tails, *marks, *consts)


def unpack(small):
    offset = 0
    pieces = []
    for extent in (D, K * CH, CH, H, H, H, DI):
        pieces.append(small[offset : offset + extent])
        offset = offset + extent
    return (
        pieces[0],
        pieces[1].reshape(K, CH),
        pieces[2],
        pieces[3],
        pieces[4],
        pieces[5],
        pieces[6],
    )


def row_marks(row_lengths, rows):
    edges = jnp.cumsum(row_lengths)
    blocks = rows // L

    def segment_at(places):
        inside = jnp.sum((places[:, None] >= edges[None, :]).astype(jnp.int32), axis=1)
        return jnp.where((places >= 0) & (places < rows), inside, -1)

    places = jnp.arange(rows, dtype=jnp.int32)
    starts = places - places % L
    segment = segment_at(places)
    before = segment_at(starts - 1)
    tail = segment_at(starts + L - 1)
    columns = [before, tail]
    columns += [segment_at(places - j) for j in range(1, K)]
    columns += [segment_at(places + j) for j in range(1, K)]
    flags = jnp.stack([(c == segment).astype(f32) for c in columns], axis=1)
    stay = (before == tail).astype(f32)[::L]
    marks = (
        flags,
        segment[:, None],
        segment.reshape(blocks, 1, L),
        jnp.broadcast_to(stay[:, None, None], (blocks, 1, LANES)),
    )
    live_rows = (places < edges[-1]).astype(f32)
    return marks, live_rows


def lanes(vector):
    return jnp.pad(vector, (0, LANES - H))[None]


def pre_norm(rows_in, gain_in):
    inv_rms = lax.rsqrt(jnp.mean(rows_in * rows_in, axis=1, keepdims=True) + EPS_NORM)
    return rows_in * inv_rms * gain_in


def adam(weight, first, second, grad_sum, step_rate, decay_on):
    first_new = BETA_ONE * first + (1.0 - BETA_ONE) * grad_sum
    second_new = BETA_TWO * second + (1.0 - BETA_TWO) * grad_sum * grad_sum
    first_hat = first_new / (1.0 - BETA_ONE**STEP)
    second_hat = second_new / (1.0 - BETA_TWO**STEP)
    weight_new = weight - step_rate * (
        first_hat / (jnp.sqrt(second_hat) + ADAM_EPS) + decay_on * weight
    )
    return (weight_new, first_new, second_new)


def total(grad):
    part = lax.psum_scatter(grad, ("shard", "rep"), scatter_dimension=0, tiled=True)
    return lax.all_gather(part, "rep", axis=0, tiled=True)


def gather(block):
    share = block.shape[0] // lax.axis_size("rep")
    own = lax.dynamic_slice_in_dim(block, lax.axis_index("rep") * share, share, 0)
    return lax.all_gather(own, ("shard", "rep"), axis=0, tiled=True)


def shards(
    tokens,
    cotangent,
    lengths,
    proj_weight,
    proj_first,
    proj_second,
    out_weight,
    out_first,
    out_second,
    small_params,
    small_first,
    small_second,
):
    rows = tokens.shape[0]
    marks, live_rows = row_marks(lengths[0], rows)
    block_rows, small_count = proj_weight.shape[0], small_params.shape[0]
    spare = block_rows * (WIDE - PROJ)
    riding = jnp.pad(small_params, (0, spare - small_count)).reshape(block_rows, WIDE - PROJ)
    proj_full = gather(jnp.concatenate([proj_weight, riding], axis=1).astype(bf16))
    out_full = gather(out_weight.astype(bf16))
    small_full = proj_full[:, PROJ:].reshape(-1, spare)[:, :small_count].reshape(-1)
    gain_in, conv_w, conv_b, step_b, rate_log, skip, gain_out = unpack(small_full.astype(f32))
    heads = jnp.pad(jnp.repeat(jnp.eye(H, dtype=bf16), P_SIZE, axis=1), ((0, LANES - H), (0, 0)))
    consts = (
        conv_w,
        conv_b[None],
        lanes(step_b),
        lanes(jnp.exp(rate_log)),
        jnp.repeat(skip, P_SIZE)[None],
        gain_out[None],
        heads,
    )
    normed, norm_back = jax.vjp(pre_norm, tokens, gain_in)
    normed_low = normed.astype(bf16)
    projected = dot(normed_low, proj_full)
    mixed_low, y, states, tails = run_forward(projected, marks, consts)
    back_grad = (live_rows[:, None] * cotangent).astype(bf16)
    out_grad = dot(mixed_low, back_grad, ((0,), (0,)))
    sum_out = total(out_grad)
    d_mixed = dot(back_grad, out_full, ((1,), (1,)))
    d_projected, gconv, ghead, gwide = run_backward(
        projected, d_mixed, y, states, tails, marks, consts
    )
    proj_grad = dot(normed_low, d_projected, ((0,), (0,)))
    sum_proj = total(proj_grad)[:, :PROJ]
    d_normed = dot(d_projected, proj_full, ((1,), (1,)))
    d_rows, d_gain = norm_back(d_normed)
    token_grad = cotangent + d_rows
    branch = dot(mixed_low, out_full)
    block_out = tokens + live_rows[:, None] * branch
    small_grad = jnp.concatenate(
        [
            d_gain,
            gconv[:K].reshape(-1),
            gconv[K],
            ghead[0, :H],
            ghead[1, :H],
            gwide[1].reshape(H, P_SIZE).sum(axis=1),
            gwide[0],
        ]
    )
    small_all = lax.psum(jnp.pad(small_grad, (0, -small_grad.shape[0] % 1024)).reshape(-1, LANES), ("rep", "shard"))
    sum_small = lax.dynamic_slice_in_dim(
        small_all.reshape(-1), lax.axis_index("shard") * small_count, small_count, 0
    )
    return (
        (block_out, token_grad)
        + adam(proj_weight, proj_first, proj_second, sum_proj, RATE_PROJ, DECAY_WEIGHT)
        + adam(out_weight, out_first, out_second, sum_out, RATE_OUT, DECAY_WEIGHT)
        + adam(small_params, small_first, small_second, sum_small, RATE_SMALL, 0.0)
    )


def solution(mesh):
    in_specs = (
        P(("rep", "shard"), None),
        P(("rep", "shard"), None),
        P(("rep", "shard"), None),
        P("shard", None),
        P("shard", None),
        P("shard", None),
        P("shard", None),
        P("shard", None),
        P("shard", None),
        P("shard"),
        P("shard"),
        P("shard"),
    )
    out_specs = (
        P(("rep", "shard"), None),
        P(("rep", "shard"), None),
        P("shard", None),
        P("shard", None),
        P("shard", None),
        P("shard", None),
        P("shard", None),
        P("shard", None),
        P("shard"),
        P("shard"),
        P("shard"),
    )
    return jax.shard_map(shards, mesh=mesh, in_specs=in_specs, out_specs=out_specs, check_vma=False)
```
